256 devices in a mesh: pair: 64 (over z, y, core), cuts: 4 (over x).
Axes of the slice: x: 4, y: 4, z: 8, core: 2. Of those that a mesh axis runs over, the one named last changes fastest.
Arguments:
- t2_tiles: bfloat16 [24576, 128, 128], P(('pair', 'cuts')), may hold values from -6 to 6
- kc_tile: int32 [24576], P(('pair', 'cuts')), may hold values from 0 to 63
- jb_tile: int32 [24576], P(('pair', 'cuts')), may hold values from 0 to 1
- tile_owner: int32 [24576, 1], P(('pair', 'cuts')), may hold values from 0 to 63; in each aligned block of 96 rows (0 to 95, 96 to 191, ...) at most 3 rows name the same one
- w_slices: bfloat16 [1024, 32768], P(None, 'cuts'), may hold values from -0.0390625 to 0.0390625
Outputs:
- cycle: bfloat16 [1024, 16384], P('cuts', 'pair')
The draws below stay inside these ranges and needn't reach their ends.
Inputs may be any that keep to these rules, and one draw needn't show every extreme that they name: `tile_owner`: in the rows of one device no owner is named more than 3 times, and in some device some owner is named exactly 3 times.
All inputs are finite; a program needn't handle non-finite values.
Results may differ from the reference program's by a relative error of at most 0.001.
Values may be sent and summed in bfloat16 or wider, within the bound.
No kernel may reach another device: no remote copies, remote signals or barrier semaphores. Data moves between devices by JAX's collectives and lax.ppermute only.
A program may use at most 192 MiB of HBM per device.

```python
import math
import jax
import jax.numpy as jnp
import numpy as np
from jax import lax

TILE = 128
ROWS = 1024
QC = 64
SP = 2
TD = 96
CAP = 3
TILES = 24576
KCOLS = 32768
N_PAIR = 64
N_CUTS = 4


def with_ends(drawn, stream_key, least, high):
    longest = drawn.shape.index(max(drawn.shape))
    spots = []
    for shift in (0, 1):
        where = [jax.random.randint(jax.random.fold_in(stream_key, axis), (), 0, length) for axis, length in enumerate(drawn.shape)]
        where[longest] = (where[longest] + shift) % drawn.shape[longest]
        spots.append(tuple(where))
    return drawn.at[spots[0]].set(least).at[spots[1]].set(high)


def block_levels(own_key, extent, cuts, smallest, largest):
    def one(axis_at, parts):
        draws = jax.random.uniform(jax.random.fold_in(jax.random.fold_in(own_key, 6), axis_at), (parts,), jnp.float32, smallest / len(cuts), largest / len(cuts))
        return jnp.repeat(jnp.exp(draws), extent[axis_at] // parts).reshape((-1,) + (1,) * (len(extent) - axis_at - 1))

    level = one(*cuts[0])
    for cut in cuts[1:]:
        level = level * one(*cut)
    return level


def shared_out(own_key, own, number, rows, number_of, top, most, slope):
    sequence = jax.random.permutation(own_key, number_of)
    packed, usual = load_shares(number_of, rows * top, most, slope, True), load_shares(number_of, rows * top, most, slope, False)
    places = jnp.arange(number_of)

    def named(sizes, offset_by):
        used = int((sizes > 0).sum())
        fixed = max(1, used // 4)
        passed = fixed + (places - fixed + offset_by * (used - fixed)) % max(1, number_of - fixed)
        return jnp.zeros((number_of,), jnp.int32).at[sequence[jnp.where(places < fixed, places, passed)]].set(jnp.asarray(sizes, jnp.int32))

    sizes = jnp.where(number % 4 == 0, named(packed, number // 4), named(usual, number - number // 4 - 1))
    mixed = jax.random.permutation(jax.random.fold_in(own, 3), number_of)
    giver, taker = mixed[0:number_of // 2 * 2:2], mixed[1:number_of // 2 * 2:2]
    room = jnp.minimum(sizes[giver] - 1, most - sizes[taker]) // 2
    room = jnp.where((giver == sequence[0]) | (taker == sequence[0]) | (sizes[taker] == 0), 0, jnp.maximum(room, 0))
    passed = jax.random.randint(jax.random.fold_in(own, 4), (number_of // 2,), 0, 1 << 20) % (room + 1)
    sizes = sizes.at[giver].add(-passed).at[taker].add(passed)
    items = jnp.searchsorted(jnp.cumsum(sizes), jnp.arange(rows * top), side="right").astype(jnp.int32)
    grid = items.reshape(top, rows).T
    grid = grid[jax.random.permutation(jax.random.fold_in(own, 1), rows)]
    offset_by = jax.random.randint(jax.random.fold_in(own, 2), (rows, 1), 0, top)
    return jnp.take_along_axis(grid, (jnp.arange(top)[None, :] + offset_by) % top, axis=1)


def load_shares(count, total, limit, skew, full):
    portions = [(1 << 20) // math.isqrt(standing ** skew) + 1 for standing in range(1, count + 1)]
    largest = limit if full else min(limit, max(-(-total // count), total * portions[0] // sum(portions)))
    least = 1 if total - largest >= count - 1 else 0
    counts, surplus = [largest] + [least] * (count - 1), total - largest - least * (count - 1)
    while surplus > 0:
        free = [i for i in range(1, count) if counts[i] < largest] or [i for i in range(1, count) if counts[i] < limit]
        mass, budget = sum([portions[i] for i in free]), surplus
        for i in free:
            addition = min(limit - counts[i], max(1, budget * portions[i] // mass), surplus)
            counts[i] = counts[i] + addition
            surplus = surplus - addition
    return np.array(counts)


def scatter_about(own_key, dims, deviation, most, split=(), kind=jnp.bfloat16):
    array = jax.random.normal(own_key, dims, jnp.float32) * deviation
    if len(split) > 0:
        array = block_levels(own_key, dims, split, -0.22, 0.18) * array
    return jnp.clip(array, min=-most, max=most).astype(kind)


def setup_inputs(seed: int = 0) -> dict:
    seeds = jax.random.split(jax.random.key(seed), 6)
    t2_tiles = scatter_about(seeds[0], (TILES, TILE, TILE), 1.0, 6.0, ((0, 256),))
    kc_tile = with_ends(jax.random.randint(seeds[1], (TILES,), 0, QC), jax.random.fold_in(seeds[1], 1), 0, QC - 1).astype(jnp.int32)
    jb_tile = with_ends(jax.random.randint(seeds[2], (TILES,), 0, SP), jax.random.fold_in(seeds[2], 1), 0, SP - 1).astype(jnp.int32)
    tile_owner_keys = jax.random.split(jax.random.fold_in(seeds[3], 1), TILES // TD)
    tile_owner_turns = jax.random.permutation(jax.random.fold_in(seeds[3], 3), TILES // TD)
    tile_owner = jax.vmap(lambda own, number: shared_out(jax.random.fold_in(seeds[3], 2), own, number, TD, N_PAIR, 1, CAP, 2))(tile_owner_keys, tile_owner_turns).reshape((TILES, 1))
    w_slices = scatter_about(seeds[4], (ROWS, KCOLS), (N_CUTS * TILE * TD // SP) ** -0.5, 0.0390625, ((1, 4),))
    return {"t2_tiles": t2_tiles, "kc_tile": kc_tile, "jb_tile": jb_tile, "tile_owner": tile_owner, "w_slices": w_slices}


def reference(t2_tiles, kc_tile, jb_tile, tile_owner, w_slices):
    tiles_all = t2_tiles.shape[0]
    cut_index = (jnp.arange(tiles_all, dtype=jnp.int32) // TD) % N_CUTS
    w_column = (cut_index * QC + kc_tile).astype(jnp.int32)
    out_column = (tile_owner[:, 0] * SP + jb_tile).astype(jnp.int32)
    w_blocks = w_slices.reshape(ROWS, N_CUTS * QC, TILE)
    block_size = 256
    turns = tiles_all // block_size

    def one_block(running, position):
        start = (position * block_size).astype(jnp.int32)
        tile_block = lax.dynamic_slice_in_dim(t2_tiles, start, block_size, 0)
        w_pick = lax.dynamic_slice_in_dim(w_column, start, block_size, 0)
        out_pick = lax.dynamic_slice_in_dim(out_column, start, block_size, 0)
        picked = jnp.take(w_blocks, w_pick, axis=1).astype(jnp.float32)
        product = jnp.einsum("rna,nab->rnb", picked, tile_block.astype(jnp.float32))
        running = running.at[:, out_pick, :].add(product)
        return running, None

    start_value = jnp.zeros((ROWS, N_PAIR * SP, TILE), jnp.float32)
    total, _ = lax.scan(one_block, start_value, jnp.arange(turns, dtype=jnp.int32))
    return total.reshape(ROWS, N_PAIR * SP * TILE).astype(jnp.bfloat16)
```

```python
import functools

import jax
import jax.numpy as jnp
from jax import lax
from jax.experimental import pallas as pl
from jax.experimental.pallas import tpu as pltpu
from jax.sharding import Mesh
from jax.sharding import PartitionSpec as P

Z, Y, K, X = 8, 4, 2, 4
GROUP = Y * K
CAP = 3
TILE = 128
STEPS = 2
CHUNKS = Z // STEPS
SLOTS = STEPS * CAP
META = 16
BLOCK = SLOTS * TILE + META
DEPTH = 8


def route_kernel(place, kc, jb, owner, tiles, *rest):
    sends = rest[:CHUNKS]
    counts, codes, metas, sem, meta_sem = rest[CHUNKS:]
    held = tiles.shape[0]
    z = place[0]

    def clear(o, carry):
        counts[o] = 0
        return carry

    lax.fori_loop(0, Z * GROUP, clear, 0)
    codes[...] = jnp.full(codes.shape, -1.0, jnp.float32)
    lane = lax.broadcasted_iota(jnp.int32, (1, TILE), 1)

    def one(i, carry):
        o = owner[i]
        rank = counts[o]
        counts[o] = rank + 1
        dest = lax.rem(o, GROUP)
        step = lax.rem(z - 1 - lax.div(o, GROUP) + 2 * Z, Z)
        chunk = lax.div(step, STEPS)
        slot = lax.rem(step, STEPS) * CAP + rank
        row = pl.multiple_of(dest * BLOCK + slot * TILE, 16)
        for c in range(CHUNKS):

            @pl.when(chunk == c)
            def _():
                pltpu.make_async_copy(tiles.at[i], sends[c].at[pl.ds(row, TILE), :], sem).start()

        line = pl.ds(chunk * GROUP + dest, 1)
        code = (kc[i] * 2 + jb[i]).astype(jnp.float32)
        codes[line, :] = jnp.where(lane == slot, code, codes[line, :])
        return carry

    lax.fori_loop(0, held, one, 0)
    metas[...] = jnp.broadcast_to(codes[...][:, None, :], metas.shape).astype(metas.dtype)
    for c in range(CHUNKS):
        for d in range(GROUP):
            pltpu.make_async_copy(
                metas.at[c * GROUP + d],
                sends[c].at[pl.ds(d * BLOCK + SLOTS * TILE, META), :],
                meta_sem.at[c * GROUP + d],
            ).start()
    for c in range(CHUNKS):
        for d in range(GROUP):
            pltpu.make_async_copy(
                metas.at[c * GROUP + d],
                sends[c].at[pl.ds(d * BLOCK + SLOTS * TILE, META), :],
                meta_sem.at[c * GROUP + d],
            ).wait()
    pltpu.make_async_copy(tiles, tiles, sem).wait()


def route(place, kc, jb, owner, tiles):
    smem = pl.BlockSpec(memory_space=pltpu.SMEM)
    hbm = pl.BlockSpec(memory_space=pl.ANY)
    return pl.pallas_call(
        route_kernel,
        out_shape=[jax.ShapeDtypeStruct((GROUP * BLOCK, TILE), tiles.dtype)] * CHUNKS,
        in_specs=[smem] * 4 + [hbm],
        out_specs=[hbm] * CHUNKS,
        scratch_shapes=[
            pltpu.SMEM((Z * GROUP,), jnp.int32),
            pltpu.VMEM((CHUNKS * GROUP, TILE), jnp.float32),
            pltpu.VMEM((CHUNKS * GROUP, META, TILE), jnp.bfloat16),
            pltpu.SemaphoreType.DMA,
            pltpu.SemaphoreType.DMA((CHUNKS * GROUP,)),
        ],
        compiler_params=pltpu.CompilerParams(vmem_limit_bytes=16 << 20),
        name="route",
    )(place, kc, jb, owner, tiles)


def contract_kernel(place, got, w, *rest):
    outs = rest[: X * STEPS]
    total, held, codes_v, codes, rows, cols, sums, code_sem, w_sem = rest[X * STEPS :]
    row_count = w.shape[0]
    part = row_count // X
    lines = [got[d * BLOCK + SLOTS * TILE : (d + 1) * BLOCK, :][0:1] for d in range(GROUP)]
    codes_v[...] = jnp.concatenate(lines, axis=0).astype(jnp.float32).astype(jnp.int32)
    copy = pltpu.make_async_copy(codes_v, codes, code_sem)
    copy.start()
    copy.wait()
    count = jnp.int32(0)
    for d in range(GROUP):
        for slot in range(SLOTS):
            code = codes[d, slot]
            rows[count] = d * BLOCK + slot * TILE
            cols[count] = lax.shift_right_arithmetic(code, 1)
            sums[count] = (slot // CAP) * 2 + (code & 1)
            count = count + jnp.where(code >= 0, 1, 0)

    def fetch(i, b):
        start = pl.multiple_of(cols[i] * TILE, TILE)
        return pltpu.make_async_copy(w.at[:, pl.ds(start, TILE)], held.at[b], w_sem.at[b])

    for b in range(DEPTH):

        @pl.when(b < count)
        def _():
            fetch(b, b).start()

    total[...] = jnp.zeros_like(total)

    def one(i, carry):
        b = lax.rem(i, DEPTH)
        fetch(i, b).wait()
        tile = got[pl.ds(pl.multiple_of(rows[i], 16), TILE), :]
        total[sums[i]] += jnp.dot(held[b], tile, preferred_element_type=jnp.float32)

        @pl.when(i + DEPTH < count)
        def _():
            fetch(i + DEPTH, b).start()

        return carry

    lax.fori_loop(0, count, one, 0)
    x = place[1]
    for away in range(X):
        first = pl.multiple_of(lax.rem(x + away, X) * part, part)
        for s in range(STEPS):
            for j in range(2):
                outs[away * STEPS + s][:, j * TILE : (j + 1) * TILE] = total[
                    s * 2 + j, pl.ds(first, part), :
                ]


def contract(place, got, w):
    smem = pl.BlockSpec(memory_space=pltpu.SMEM)
    vmem = pl.BlockSpec(memory_space=pltpu.VMEM)
    row_count = w.shape[0]
    most = GROUP * SLOTS
    return pl.pallas_call(
        contract_kernel,
        out_shape=[jax.ShapeDtypeStruct((row_count // X, 2 * TILE), jnp.float32)] * (X * STEPS),
        in_specs=[smem, vmem, pl.BlockSpec(memory_space=pl.ANY)],
        out_specs=[vmem] * (X * STEPS),
        scratch_shapes=[
            pltpu.VMEM((2 * STEPS, row_count, TILE), jnp.float32),
            pltpu.VMEM((DEPTH, row_count, TILE), jnp.bfloat16),
            pltpu.VMEM((GROUP, TILE), jnp.int32),
            pltpu.SMEM((GROUP, TILE), jnp.int32),
            pltpu.SMEM((most + 1,), jnp.int32),
            pltpu.SMEM((most + 1,), jnp.int32),
            pltpu.SMEM((most + 1,), jnp.int32),
            pltpu.SemaphoreType.DMA,
            pltpu.SemaphoreType.DMA((DEPTH,)),
        ],
        compiler_params=pltpu.CompilerParams(vmem_limit_bytes=24 << 20),
        cost_estimate=pl.CostEstimate(
            flops=most * row_count * TILE * TILE, bytes_accessed=16 << 20, transcendentals=0
        ),
        name="contract",
    )(place, got, w)


def local(t2_tiles, kc_tile, jb_tile, tile_owner, w_slices):
    z, x = lax.axis_index("z"), lax.axis_index("x")
    place = jnp.stack([z, x]).astype(jnp.int32)
    up_x = [(i, (i + 1) % X) for i in range(X)]
    down_x = [(i, (i - 1) % X) for i in range(X)]
    up_z = [(i, (i + 1) % Z) for i in range(Z)]
    sends = route(place, kc_tile, jb_tile, tile_owner[:, 0], t2_tiles)
    gots = [lax.all_to_all(s, ("y", "k"), split_axis=0, concat_axis=0, tiled=True) for s in sends]
    running = None
    for c in range(CHUNKS):
        own_a, own_b, next_a, next_b, far_a, far_b, last_a, last_b = contract(
            place, gots[c], w_slices
        )
        from_low_far = lax.ppermute(far_b, "x", up_x)
        from_high_far = lax.ppermute(far_a, "x", down_x)
        from_low_a = lax.ppermute(next_a, "x", up_x)
        from_high_b = lax.ppermute(last_b, "x", down_x)
        from_low_b = lax.ppermute(next_b + from_low_far, "x", up_x)
        from_high_a = lax.ppermute(last_a + from_high_far, "x", down_x)
        first = own_a + from_low_a + from_high_a
        if running is not None:
            first = first + running
        second = own_b + from_low_b + from_high_b + lax.ppermute(first, "z", up_z)
        if c < CHUNKS - 1:
            running = lax.ppermute(second, "z", up_z)
    return second.astype(jnp.bfloat16)


def solution(mesh):
    fine = Mesh(mesh.devices.reshape(Z, Y, K, X), ("z", "y", "k", "x"))
    pair = ("z", "y", "k")
    every = ("z", "y", "k", "x")
    return jax.shard_map(
        local,
        mesh=fine,
        in_specs=(
            P(every, None, None),
            P(every),
            P(every),
            P(every, None),
            P(None, "x"),
        ),
        out_specs=P("x", pair),
        check_vma=False,
    )
```

```python
import jax
import jax.numpy as jnp
from jax import lax
from jax.experimental import pallas as pl
from jax.experimental.pallas import tpu as pltpu
from jax.sharding import Mesh
from jax.sharding import PartitionSpec as P

HIGH, LOW, Y, K, X = 4, 2, 4, 2, 4
GROUP = LOW * Y * K
CAP = 3
TILE = 128
META = 16
DEPTH = 4
WIDE = 4
ORDER = (2, 1, 3, 0)
CHUNKS = (4,)
FIRST = (0,)
CALLS = ((0, 0, 2), (0, 2, 2))


def slots_of(steps):
    return steps * CAP


def block_of(steps):
    return slots_of(steps) * TILE + META


def route_kernel(chunk, kc, jb, owner, tiles, send, *scratch):
    kc_s, jb_s, owner_s, counts, codes, kind_sem, sem = scratch
    held = tiles.shape[0]
    steps = CHUNKS[chunk]
    loads = [
        pltpu.make_async_copy(a, b, kind_sem.at[i])
        for i, (a, b) in enumerate(((kc, kc_s), (jb, jb_s), (owner, owner_s)))
    ]
    for load in loads:
        load.start()

    def clear(o, carry):
        counts[o] = 0
        return carry

    lax.fori_loop(0, HIGH * GROUP, clear, 0)
    codes[...] = jnp.full(codes.shape, -1.0, jnp.float32)
    lane = lax.broadcasted_iota(jnp.int32, (1, TILE), 1)
    high = lax.axis_index("zh")
    for load in loads:
        load.wait()

    def one(i, sent):
        name = owner_s[i]
        away = (lax.shift_right_logical(name, 4) - high) & (HIGH - 1)
        step = jnp.int32(-1)
        for s in range(steps):
            step = jnp.where(away == ORDER[FIRST[chunk] + s], s, step)

        @pl.when(step >= 0)
        def _():
            rank = counts[name]
            counts[name] = rank + 1
            dest = name & (GROUP - 1)
            slot = step * CAP + rank
            row = pl.multiple_of(slot * TILE, TILE)
            pltpu.make_async_copy(tiles.at[i], send.at[dest, pl.ds(row, TILE), :], sem).start()
            line = pl.ds(dest, 1)
            code = (kc_s[i] * 2 + jb_s[i]).astype(jnp.float32)
            codes[line, :] = jnp.where(lane == slot, code, codes[line, :])

        return sent + jnp.where(step >= 0, 1, 0)

    sent = lax.fori_loop(0, held, one, 0)
    send[:, slots_of(steps) * TILE :, :] = jnp.broadcast_to(
        codes[...][:, None, :], (GROUP, META, TILE)
    ).astype(send.dtype)

    def arrived(i, carry):
        pltpu.make_async_copy(tiles.at[0], send.at[0, pl.ds(0, TILE), :], sem).wait()
        return carry

    lax.fori_loop(0, sent, arrived, 0)


def route(chunk, kc, jb, owner, tiles):
    hbm = pl.BlockSpec(memory_space=pltpu.HBM)
    held = tiles.shape[0]

    def kernel(*refs):
        route_kernel(chunk, *refs)

    return pl.pallas_call(
        kernel,
        out_shape=jax.ShapeDtypeStruct((GROUP, block_of(CHUNKS[chunk]), TILE), tiles.dtype),
        in_specs=[hbm] * 4,
        out_specs=pl.BlockSpec(memory_space=pltpu.VMEM),
        scratch_shapes=[
            pltpu.SMEM((held,), jnp.int32),
            pltpu.SMEM((held,), jnp.int32),
            pltpu.SMEM((held,), jnp.int32),
            pltpu.SMEM((HIGH * GROUP,), jnp.int32),
            pltpu.VMEM((GROUP, TILE), jnp.float32),
            pltpu.SemaphoreType.DMA((3,)),
            pltpu.SemaphoreType.DMA,
        ],
        compiler_params=pltpu.CompilerParams(vmem_limit_bytes=60 << 20),
        cost_estimate=pl.CostEstimate(flops=0, bytes_accessed=8 << 20, transcendentals=0),
        name="route",
    )(kc, jb, owner, tiles)


def contract_kernel(begin, steps, got, w, *rest):
    outs = rest[:6]
    tiles, total, held, codes_b, codes_v, codes, rows, cols, sums, sems, w_sem = rest[6:]
    row_count = w.shape[0]
    half = row_count // X // 2
    slots = slots_of(steps)
    zero = GROUP * slots
    metas = pltpu.make_async_copy(got.at[:, pl.ds(got.shape[1] - META, META), :], codes_b, sems.at[0])
    metas.start()
    arrives = []
    for j in range(GROUP):
        arrives.append(
            pltpu.make_async_copy(
                got.at[j, pl.ds(begin * CAP * TILE, slots * TILE), :],
                tiles.at[pl.ds(j * slots * TILE, slots * TILE), :],
                sems.at[2 + j],
            )
        )
    for arrive in arrives:
        arrive.start()
    tiles[zero * TILE :, :] = jnp.zeros((TILE, TILE), tiles.dtype)
    metas.wait()
    codes_v[...] = codes_b[...][:, 0, :].astype(jnp.float32).astype(jnp.int32)
    copy = pltpu.make_async_copy(codes_v, codes, sems.at[1])
    copy.start()
    total[...] = jnp.zeros_like(total)
    copy.wait()
    count = jnp.int32(0)
    for which in range(2 * steps):
        for j in range(GROUP):
            for rank in range(CAP):
                slot = which // 2 * CAP + rank
                code = codes[j, begin * CAP + slot]
                rows[count] = (j * slots + slot) * TILE
                cols[count] = lax.shift_right_arithmetic(code, 1) * TILE
                sums[count] = which
                count = count + jnp.where((code >= 0) & ((code & 1) == which % 2), 1, 0)
        for _ in range(WIDE - 1):
            rows[count] = zero * TILE
            cols[count] = 0
            sums[count] = which
            count = count + jnp.where(lax.rem(count, WIDE) > 0, 1, 0)
    bunches = lax.div(count, WIDE)

    def fetch(i, b, side):
        start = pl.multiple_of(cols[WIDE * i + side], TILE)
        return pltpu.make_async_copy(
            w.at[:, pl.ds(start, TILE)],
            held.at[b, :, pl.ds(side * TILE, TILE)],
            w_sem.at[b, side],
        )

    for b in range(DEPTH):

        @pl.when(b < bunches)
        def _():
            for side in range(WIDE):
                fetch(b, b, side).start()

    for arrive in arrives:
        arrive.wait()

    def one(i, carry):
        b = lax.rem(i, DEPTH)
        for side in range(WIDE):
            fetch(i, b, side).wait()
        picked = [
            tiles[pl.ds(pl.multiple_of(rows[WIDE * i + side], TILE), TILE), :]
            for side in range(WIDE)
        ]
        total[sums[WIDE * i]] += jnp.dot(
            held[b], jnp.concatenate(picked, axis=0), preferred_element_type=jnp.float32
        )

        @pl.when(i + DEPTH < bunches)
        def _():
            for side in range(WIDE):
                fetch(i + DEPTH, b, side).start()

        return carry

    lax.fori_loop(0, bunches, one, 0)
    own_a, own_b, up, down, next_b, last_a = outs
    x = lax.axis_index("x")

    def give(ref, at, away, side):
        first = lax.rem(x + away, X) * (2 * half) + side * half
        first = pl.multiple_of(first, half)
        for s in range(steps):
            for j in range(2):
                ref[at + s * half : at + (s + 1) * half, j * TILE : (j + 1) * TILE] = total[
                    s * 2 + j, pl.ds(first, half), :
                ]

    give(up, 0, 2, 1)
    give(up, steps * half, 1, 0)
    give(down, 0, 2, 0)
    give(down, steps * half, 3, 1)
    give(next_b, 0, 1, 1)
    give(last_a, 0, 3, 0)
    give(own_a, 0, 0, 0)
    give(own_b, 0, 0, 1)


def contract(begin, steps, got, w):
    vmem = pl.BlockSpec(memory_space=pltpu.VMEM)
    hbm = pl.BlockSpec(memory_space=pltpu.HBM)
    row_count = w.shape[0]
    half = row_count // X // 2
    slots = slots_of(steps)
    most = GROUP * slots + 2 * steps * WIDE
    one = jax.ShapeDtypeStruct((steps * half, 2 * TILE), jnp.float32)
    two = jax.ShapeDtypeStruct((2 * steps * half, 2 * TILE), jnp.float32)

    def kernel(*refs):
        contract_kernel(begin, steps, *refs)

    return pl.pallas_call(
        kernel,
        out_shape=[one, one, two, two, one, one],
        in_specs=[hbm, hbm],
        out_specs=[vmem] * 6,
        scratch_shapes=[
            pltpu.VMEM(((GROUP * slots + 1) * TILE, TILE), jnp.bfloat16),
            pltpu.VMEM((2 * steps, row_count, TILE), jnp.float32),
            pltpu.VMEM((DEPTH, row_count, WIDE * TILE), jnp.bfloat16),
            pltpu.VMEM((GROUP, META, TILE), jnp.bfloat16),
            pltpu.VMEM((GROUP, TILE), jnp.int32),
            pltpu.SMEM((GROUP, TILE), jnp.int32),
            pltpu.SMEM((most,), jnp.int32),
            pltpu.SMEM((most,), jnp.int32),
            pltpu.SMEM((most,), jnp.int32),
            pltpu.SemaphoreType.DMA((2 + GROUP,)),
            pltpu.SemaphoreType.DMA((DEPTH, WIDE)),
        ],
        compiler_params=pltpu.CompilerParams(vmem_limit_bytes=56 << 20),
        cost_estimate=pl.CostEstimate(flops=1 << 20, bytes_accessed=1 << 20, transcendentals=0),
        name="contract",
    )(got, w)


def local(t2_tiles, kc_tile, jb_tile, tile_owner, w_slices):
    half = w_slices.shape[0] // X // 2
    up_x = [(i, (i + 1) % X) for i in range(X)]
    down_x = [(i, (i - 1) % X) for i in range(X)]
    names = tile_owner.reshape(-1)
    gots = []
    for chunk in range(len(CHUNKS)):
        sent = route(chunk, kc_tile, jb_tile, names, t2_tiles)
        gots.append(lax.all_to_all(sent, ("zl", "y", "k"), split_axis=0, concat_axis=0, tiled=True))
    parts, before = [], []
    for chunk, begin, steps in CALLS:
        cut = steps * half
        got = lax.optimization_barrier((gots[chunk], *before))[0]
        own_a, own_b, up, down, next_b, last_a = contract(begin, steps, got, w_slices)
        from_low = lax.ppermute(up, "x", up_x)
        from_high = lax.ppermute(down, "x", down_x)
        next_b, last_a = next_b + from_low[:cut], last_a + from_high[:cut]
        before = [next_b, last_a]
        from_low_b = lax.ppermute(next_b, "x", up_x)
        from_high_a = lax.ppermute(last_a, "x", down_x)
        for s in range(steps):
            here = slice(s * half, (s + 1) * half)
            there = slice(cut + s * half, cut + (s + 1) * half)
            block_a = own_a[here] + from_low[there] + from_high_a[here]
            block_b = own_b[here] + from_high[there] + from_low_b[here]
            block = jnp.concatenate([block_a, block_b], axis=0)
            away = ORDER[FIRST[chunk] + begin + s]
            if away:
                block = lax.ppermute(block, "zh", [(i, (i + away) % HIGH) for i in range(HIGH)])
            parts.append(block)
    return sum(parts[1:], parts[0]).astype(jnp.bfloat16)


def solution(mesh):
    every = ("zh", "zl", "y", "k", "x")
    fine = Mesh(mesh.devices.reshape(HIGH, LOW, Y, K, X), every)
    return jax.shard_map(
        local,
        mesh=fine,
        in_specs=(
            P(every, None, None),
            P(every),
            P(every),
            P(every, None),
            P(None, "x"),
        ),
        out_specs=P("x", every[:4]),
        check_vma=False,
    )
```

```python
import jax
import jax.numpy as jnp
from jax import lax
from jax.experimental import pallas as pl
from jax.experimental.pallas import tpu as pltpu
from jax.sharding import Mesh
from jax.sharding import PartitionSpec as P

HIGH, LOW, Y, K, X = 4, 2, 4, 2, 4
GROUP = LOW * Y * K
CAP = 3
TILE = 128
META = 16
DEPTH = 4
WIDE = 4
ORDER = (2, 1, 3, 0)
CHUNKS = (3, 1)
FIRST = (0, 3)


def slots_of(steps):
    return steps * CAP


def block_of(steps):
    return slots_of(steps) * TILE + META


def route_kernel(kc, jb, owner, tiles, *rest):
    sends, scratch = rest[: len(CHUNKS)], rest[len(CHUNKS) :]
    kc_s, jb_s, owner_s, counts, codes, kind_sem, sem = scratch
    held = tiles.shape[0]
    loads = [
        pltpu.make_async_copy(a, b, kind_sem.at[i])
        for i, (a, b) in enumerate(((kc, kc_s), (jb, jb_s), (owner, owner_s)))
    ]
    for load in loads:
        load.start()

    def clear(o, carry):
        counts[o] = 0
        return carry

    lax.fori_loop(0, HIGH * GROUP, clear, 0)
    codes[...] = jnp.full(codes.shape, -1.0, jnp.float32)
    lane = lax.broadcasted_iota(jnp.int32, (1, TILE), 1)
    high = lax.axis_index("zh")
    for load in loads:
        load.wait()

    def one(i, carry):
        name = owner_s[i]
        away = (lax.shift_right_logical(name, 4) - high) & (HIGH - 1)
        step = jnp.int32(0)
        for s in range(1, HIGH):
            step = jnp.where(away == ORDER[s], s, step)
        rank = counts[name]
        counts[name] = rank + 1
        dest = name & (GROUP - 1)
        for c, send in enumerate(sends):

            @pl.when((step >= FIRST[c]) & (step < FIRST[c] + CHUNKS[c]))
            def _():
                row = pl.multiple_of(((step - FIRST[c]) * CAP + rank) * TILE, TILE)
                pltpu.make_async_copy(tiles.at[i], send.at[dest, pl.ds(row, TILE), :], sem).start()

        line = pl.ds(dest, 1)
        code = (kc_s[i] * 2 + jb_s[i]).astype(jnp.float32)
        codes[line, :] = jnp.where(lane == step * CAP + rank, code, codes[line, :])
        return carry

    lax.fori_loop(0, held, one, 0)
    for c, send in enumerate(sends):
        found = codes[...]
        if FIRST[c]:
            found = pltpu.roll(found, TILE - FIRST[c] * CAP, axis=1)
        send[:, slots_of(CHUNKS[c]) * TILE :, :] = jnp.broadcast_to(
            found[:, None, :], (GROUP, META, TILE)
        ).astype(send.dtype)
    pltpu.make_async_copy(tiles, tiles, sem).wait()


def route(kc, jb, owner, tiles):
    hbm = pl.BlockSpec(memory_space=pltpu.HBM)
    held = tiles.shape[0]
    return pl.pallas_call(
        route_kernel,
        out_shape=[jax.ShapeDtypeStruct((GROUP, block_of(n), TILE), tiles.dtype) for n in CHUNKS],
        in_specs=[hbm] * 4,
        out_specs=[pl.BlockSpec(memory_space=pltpu.VMEM)] * len(CHUNKS),
        scratch_shapes=[
            pltpu.SMEM((held,), jnp.int32),
            pltpu.SMEM((held,), jnp.int32),
            pltpu.SMEM((held,), jnp.int32),
            pltpu.SMEM((HIGH * GROUP,), jnp.int32),
            pltpu.VMEM((GROUP, TILE), jnp.float32),
            pltpu.SemaphoreType.DMA((3,)),
            pltpu.SemaphoreType.DMA,
        ],
        compiler_params=pltpu.CompilerParams(vmem_limit_bytes=60 << 20),
        cost_estimate=pl.CostEstimate(flops=0, bytes_accessed=8 << 20, transcendentals=0),
        name="route",
    )(kc, jb, owner, tiles)


def contract_kernel(steps, direct, got, w, *rest):
    many = 4 if direct else 6
    outs = rest[:many]
    tiles, total, held, codes_b, codes_v, codes, rows, cols, sums, sems, w_sem = rest[many:]
    row_count = w.shape[0]
    half = row_count // X // 2
    slots = slots_of(steps)
    zero = GROUP * slots
    metas = pltpu.make_async_copy(got.at[:, pl.ds(got.shape[1] - META, META), :], codes_b, sems.at[0])
    metas.start()
    arrives = []
    for j in range(GROUP):
        arrives.append(
            pltpu.make_async_copy(
                got.at[j, pl.ds(0, slots * TILE), :],
                tiles.at[pl.ds(j * slots * TILE, slots * TILE), :],
                sems.at[2 + j],
            )
        )
    for arrive in arrives:
        arrive.start()
    tiles[zero * TILE :, :] = jnp.zeros((TILE, TILE), tiles.dtype)
    metas.wait()
    codes_v[...] = codes_b[...][:, 0, :].astype(jnp.float32).astype(jnp.int32)
    copy = pltpu.make_async_copy(codes_v, codes, sems.at[1])
    copy.start()
    total[...] = jnp.zeros_like(total)
    copy.wait()
    count = jnp.int32(0)
    for which in range(2 * steps):
        for j in range(GROUP):
            for rank in range(CAP):
                slot = which // 2 * CAP + rank
                code = codes[j, slot]
                rows[count] = (j * slots + slot) * TILE
                cols[count] = lax.shift_right_arithmetic(code, 1) * TILE
                sums[count] = which
                count = count + jnp.where((code >= 0) & ((code & 1) == which % 2), 1, 0)
        for _ in range(WIDE - 1):
            rows[count] = zero * TILE
            cols[count] = 0
            sums[count] = which
            count = count + jnp.where(lax.rem(count, WIDE) > 0, 1, 0)
    bunches = lax.div(count, WIDE)

    def fetch(i, b, side):
        start = pl.multiple_of(cols[WIDE * i + side], TILE)
        return pltpu.make_async_copy(
            w.at[:, pl.ds(start, TILE)],
            held.at[b, :, pl.ds(side * TILE, TILE)],
            w_sem.at[b, side],
        )

    for b in range(DEPTH):

        @pl.when(b < bunches)
        def _():
            for side in range(WIDE):
                fetch(b, b, side).start()

    for arrive in arrives:
        arrive.wait()

    def one(i, carry):
        b = lax.rem(i, DEPTH)
        for side in range(WIDE):
            fetch(i, b, side).wait()
        picked = [
            tiles[pl.ds(pl.multiple_of(rows[WIDE * i + side], TILE), TILE), :]
            for side in range(WIDE)
        ]
        total[sums[WIDE * i]] += jnp.dot(
            held[b], jnp.concatenate(picked, axis=0), preferred_element_type=jnp.float32
        )

        @pl.when(i + DEPTH < bunches)
        def _():
            for side in range(WIDE):
                fetch(i + DEPTH, b, side).start()

        return carry

    lax.fori_loop(0, bunches, one, 0)
    x = lax.axis_index("x")

    def give(ref, at, away, side):
        first = lax.rem(x + away, X) * (2 * half) + side * half
        first = pl.multiple_of(first, half)
        for s in range(steps):
            for j in range(2):
                ref[at + s * half : at + (s + 1) * half, j * TILE : (j + 1) * TILE] = total[
                    s * 2 + j, pl.ds(first, half), :
                ]

    if direct:
        for away in range(X):
            give(outs[away], 0, away, 0)
            give(outs[away], steps * half, away, 1)
        return
    own_a, own_b, up, down, next_b, last_a = outs
    give(up, 0, 2, 1)
    give(up, steps * half, 1, 0)
    give(down, 0, 2, 0)
    give(down, steps * half, 3, 1)
    give(next_b, 0, 1, 1)
    give(last_a, 0, 3, 0)
    give(own_a, 0, 0, 0)
    give(own_b, 0, 0, 1)


def contract(steps, direct, got, w):
    vmem = pl.BlockSpec(memory_space=pltpu.VMEM)
    hbm = pl.BlockSpec(memory_space=pltpu.HBM)
    row_count = w.shape[0]
    half = row_count // X // 2
    slots = slots_of(steps)
    most = GROUP * slots + 2 * steps * WIDE
    one = jax.ShapeDtypeStruct((steps * half, 2 * TILE), jnp.float32)
    two = jax.ShapeDtypeStruct((2 * steps * half, 2 * TILE), jnp.float32)

    outs = [two] * X if direct else [one, one, two, two, one, one]

    def kernel(*refs):
        contract_kernel(steps, direct, *refs)

    return pl.pallas_call(
        kernel,
        out_shape=outs,
        in_specs=[hbm, hbm],
        out_specs=[vmem] * len(outs),
        scratch_shapes=[
            pltpu.VMEM(((GROUP * slots + 1) * TILE, TILE), jnp.bfloat16),
            pltpu.VMEM((2 * steps, row_count, TILE), jnp.float32),
            pltpu.VMEM((DEPTH, row_count, WIDE * TILE), jnp.bfloat16),
            pltpu.VMEM((GROUP, META, TILE), jnp.bfloat16),
            pltpu.VMEM((GROUP, TILE), jnp.int32),
            pltpu.SMEM((GROUP, TILE), jnp.int32),
            pltpu.SMEM((most,), jnp.int32),
            pltpu.SMEM((most,), jnp.int32),
            pltpu.SMEM((most,), jnp.int32),
            pltpu.SemaphoreType.DMA((2 + GROUP,)),
            pltpu.SemaphoreType.DMA((DEPTH, WIDE)),
        ],
        compiler_params=pltpu.CompilerParams(vmem_limit_bytes=56 << 20),
        cost_estimate=pl.CostEstimate(flops=1 << 20, bytes_accessed=1 << 20, transcendentals=0),
        name="contract",
    )(got, w)


def local(t2_tiles, kc_tile, jb_tile, tile_owner, w_slices):
    half = w_slices.shape[0] // X // 2
    up_x = [(i, (i + 1) % X) for i in range(X)]
    down_x = [(i, (i - 1) % X) for i in range(X)]
    names = tile_owner.reshape(-1)
    gots = [
        lax.all_to_all(sent, ("zl", "y", "k"), split_axis=0, concat_axis=0, tiled=True)
        for sent in route(kc_tile, jb_tile, names, t2_tiles)
    ]

    def join(steps, sums):
        own_a, own_b, up, down, next_b, last_a = sums
        cut = steps * half
        from_low = lax.ppermute(up, "x", up_x)
        from_high = lax.ppermute(down, "x", down_x)
        next_b, last_a = next_b + from_low[:cut], last_a + from_high[:cut]
        return next_b, last_a, own_a, own_b, from_low, from_high

    def blocks(steps, joined):
        next_b, last_a, own_a, own_b, from_low, from_high = joined
        from_low_b = lax.ppermute(next_b, "x", up_x)
        from_high_a = lax.ppermute(last_a, "x", down_x)
        done = []
        for s in range(steps):
            here = slice(s * half, (s + 1) * half)
            there = slice((steps + s) * half, (steps + s + 1) * half)
            block_a = own_a[here] + from_low[there] + from_high_a[here]
            block_b = own_b[here] + from_high[there] + from_low_b[here]
            done.append(jnp.concatenate([block_a, block_b], axis=0))
        return done

    def send(block, away):
        if not away:
            return block
        return lax.ppermute(block, "zh", [(i, (i + away) % HIGH) for i in range(HIGH)])

    steps = CHUNKS[0]
    first = contract(steps, False, gots[0], w_slices)
    own, after, far, behind = contract(CHUNKS[1], True, gots[1], w_slices)
    first = join(steps, first)
    low_b, high_a, after, behind, far = lax.optimization_barrier((*first[:2], after, behind, far))
    early = blocks(steps, (low_b, high_a, *first[2:]))
    parts = [send(b, ORDER[s]) for s, b in enumerate(early)]
    parts += [own, lax.ppermute(after, "x", up_x), lax.ppermute(behind, "x", down_x)]
    parts += [lax.ppermute(far, "x", [(i, (i + 2) % X) for i in range(X)])]
    return sum(parts[1:], parts[0]).astype(jnp.bfloat16)


def solution(mesh):
    every = ("zh", "zl", "y", "k", "x")
    fine = Mesh(mesh.devices.reshape(HIGH, LOW, Y, K, X), every)
    return jax.shard_map(
        local,
        mesh=fine,
        in_specs=(
            P(every, None, None),
            P(every),
            P(every),
            P(every, None),
            P(None, "x"),
        ),
        out_specs=P("x", every[:4]),
        check_vma=False,
    )
```

```python
import jax
import jax.numpy as jnp
from jax import lax
from jax.experimental import pallas as pl
from jax.experimental.pallas import tpu as pltpu
from jax.sharding import Mesh
from jax.sharding import PartitionSpec as P

HIGH, LOW, Y, K, X = 4, 2, 4, 2, 4
GROUP = LOW * Y * K
CAP = 3
TILE = 128
META = 16
DEPTH = 4
WIDE = 4
PARTS = 4
ORDER = (2, 1, 3, 0)
CHUNKS = (3, 1)
FIRST = (0, 3)


def slots_of(steps):
    return steps * CAP


def block_of(steps):
    return slots_of(steps) * TILE + META


def route_kernel(kc, jb, owner, tiles, *rest):
    sends, scratch = rest[: len(CHUNKS)], rest[len(CHUNKS) :]
    kc_s, jb_s, owner_s, counts, codes, metas, stage, kind_sem, stage_sem, meta_sem, sem = scratch
    held = tiles.shape[0]
    part = held // PARTS

    def load_part(p):
        some = pl.ds(p * part, part)
        return pltpu.make_async_copy(tiles.at[some], stage.at[some], stage_sem.at[p])

    loads = [
        pltpu.make_async_copy(a, b, kind_sem.at[i])
        for i, (a, b) in enumerate(((kc, kc_s), (jb, jb_s), (owner, owner_s)))
    ]
    for load in loads:
        load.start()
    for p in range(PARTS):
        load_part(p).start()

    def clear(o, carry):
        counts[o] = 0
        return carry

    lax.fori_loop(0, HIGH * GROUP, clear, 0)
    codes[...] = jnp.full(codes.shape, -1.0, jnp.float32)
    lane = lax.broadcasted_iota(jnp.int32, (1, TILE), 1)
    high = lax.axis_index("zh")
    for load in loads:
        load.wait()

    def one(i, carry):
        name = owner_s[i]
        away = (lax.shift_right_logical(name, 4) - high) & (HIGH - 1)
        step = jnp.int32(0)
        for s in range(1, HIGH):
            step = jnp.where(away == ORDER[s], s, step)
        rank = counts[name]
        counts[name] = rank + 1
        dest = name & (GROUP - 1)
        for c, send in enumerate(sends):

            @pl.when((step >= FIRST[c]) & (step < FIRST[c] + CHUNKS[c]))
            def _():
                row = pl.multiple_of(((step - FIRST[c]) * CAP + rank) * TILE, TILE)
                pltpu.make_async_copy(stage.at[i], send.at[dest, pl.ds(row, TILE), :], sem).start()

        line = pl.ds(dest, 1)
        code = (kc_s[i] * 2 + jb_s[i]).astype(jnp.float32)
        codes[line, :] = jnp.where(lane == step * CAP + rank, code, codes[line, :])
        return carry

    for p in range(PARTS):
        load_part(p).wait()
        lax.fori_loop(p * part, (p + 1) * part, one, 0)
    copies = []
    for c, send in enumerate(sends):
        found = codes[...]
        if FIRST[c]:
            found = pltpu.roll(found, TILE - FIRST[c] * CAP, axis=1)
        metas[c] = jnp.broadcast_to(found[:, None, :], (GROUP, META, TILE)).astype(metas.dtype)
        there = send.at[:, pl.ds(slots_of(CHUNKS[c]) * TILE, META), :]
        copies.append(pltpu.make_async_copy(metas.at[c], there, meta_sem.at[c]))
    for copy in copies:
        copy.start()
    for copy in copies:
        copy.wait()
    pltpu.make_async_copy(stage, stage, sem).wait()


def route(kc, jb, owner, tiles):
    hbm = pl.BlockSpec(memory_space=pltpu.HBM)
    held = tiles.shape[0]
    return pl.pallas_call(
        route_kernel,
        out_shape=[jax.ShapeDtypeStruct((GROUP, block_of(n), TILE), tiles.dtype) for n in CHUNKS],
        in_specs=[hbm] * 4,
        out_specs=[hbm] * len(CHUNKS),
        scratch_shapes=[
            pltpu.SMEM((held,), jnp.int32),
            pltpu.SMEM((held,), jnp.int32),
            pltpu.SMEM((held,), jnp.int32),
            pltpu.SMEM((HIGH * GROUP,), jnp.int32),
            pltpu.VMEM((GROUP, TILE), jnp.float32),
            pltpu.VMEM((len(CHUNKS), GROUP, META, TILE), tiles.dtype),
            pltpu.VMEM(tiles.shape, tiles.dtype),
            pltpu.SemaphoreType.DMA((3,)),
            pltpu.SemaphoreType.DMA((PARTS,)),
            pltpu.SemaphoreType.DMA((len(CHUNKS),)),
            pltpu.SemaphoreType.DMA,
        ],
        compiler_params=pltpu.CompilerParams(vmem_limit_bytes=60 << 20),
        cost_estimate=pl.CostEstimate(flops=0, bytes_accessed=8 << 20, transcendentals=0),
        name="route",
    )(kc, jb, owner, tiles)


def contract_kernel(steps, direct, got, w, *rest):
    many = 4 if direct else 6
    outs = rest[:many]
    tiles, total, held, codes_b, codes_v, codes, work, sems, w_sem = rest[many:]
    row_count = w.shape[0]
    half = row_count // X // 2
    deep = CAP * TILE
    metas = pltpu.make_async_copy(got.at[:, pl.ds(got.shape[1] - META, META), :], codes_b, sems.at[0])
    metas.start()

    def arrive(s):
        here = got.at[:, pl.ds(s * deep, deep), :]
        return pltpu.make_async_copy(here, tiles.at[pl.ds(s * GROUP, GROUP)], sems.at[2 + s])

    for s in range(steps):
        arrive(s).start()
    tiles[steps * GROUP] = jnp.zeros((deep, TILE), tiles.dtype)
    metas.wait()
    codes_v[...] = codes_b[...][:, 0, :].astype(jnp.float32).astype(jnp.int32)
    copy = pltpu.make_async_copy(codes_v, codes, sems.at[1])
    copy.start()
    total[...] = jnp.zeros_like(total)
    copy.wait()

    def fetch(i, b, side):
        start = pl.multiple_of(lax.shift_right_logical(work[WIDE * i + side], 10) * TILE, TILE)
        return pltpu.make_async_copy(
            w.at[:, pl.ds(start, TILE)],
            held.at[b, :, pl.ds(side * TILE, TILE)],
            w_sem.at[b, side],
        )

    def fetch_first(least, most):
        for b in range(DEPTH):

            @pl.when((b >= least) & (b < most))
            def _():
                for side in range(WIDE):
                    fetch(b, b, side).start()

    count = jnp.int32(0)
    bounds = [jnp.int32(0)]
    for which in range(2 * steps):
        for j in range(GROUP):
            for rank in range(CAP):
                code = codes[j, which // 2 * CAP + rank]
                place = (which // 2 * GROUP + j) * 4 + rank
                work[count] = lax.shift_left(lax.shift_right_arithmetic(code, 1), 10) + place
                count = count + jnp.where((code >= 0) & ((code & 1) == which % 2), 1, 0)
        for _ in range(WIDE - 1):
            work[count] = steps * GROUP * 4
            count = count + jnp.where(lax.rem(count, WIDE) > 0, 1, 0)
        bounds.append(lax.div(count, WIDE))
        if which == 1:
            fetch_first(0, bounds[2])
    bunches = bounds[-1]
    if steps > 1:
        fetch_first(bounds[2], bunches)

    def picked(i, side):
        place = work[WIDE * i + side] & 1023
        row = pl.multiple_of((place & 3) * TILE, TILE)
        return tiles[lax.shift_right_logical(place, 2), pl.ds(row, TILE), :]

    for s in range(steps):
        arrive(s).wait()

        def one(i, carry, s=s):
            b = lax.rem(i, DEPTH)
            for side in range(WIDE):
                fetch(i, b, side).wait()
            right = jnp.concatenate([picked(i, side) for side in range(WIDE)], axis=0)
            which = 2 * s + jnp.where(i >= bounds[2 * s + 1], 1, 0)
            total[which] += jnp.dot(held[b], right, preferred_element_type=jnp.float32)

            @pl.when(i + DEPTH < bunches)
            def _():
                for side in range(WIDE):
                    fetch(i + DEPTH, b, side).start()

            return carry

        lax.fori_loop(bounds[2 * s], bounds[2 * s + 2], one, 0)
    x = lax.axis_index("x")

    def give(ref, at, away, side):
        first = lax.rem(x + away, X) * (2 * half) + side * half
        first = pl.multiple_of(first, half)
        for s in range(steps):
            for j in range(2):
                ref[at + s * half : at + (s + 1) * half, j * TILE : (j + 1) * TILE] = total[
                    s * 2 + j, pl.ds(first, half), :
                ]

    if direct:
        for away in range(X):
            give(outs[away], 0, away, 0)
            give(outs[away], steps * half, away, 1)
        return
    own_a, own_b, up, down, next_b, last_a = outs
    give(up, 0, 2, 1)
    give(up, steps * half, 1, 0)
    give(down, 0, 2, 0)
    give(down, steps * half, 3, 1)
    give(next_b, 0, 1, 1)
    give(last_a, 0, 3, 0)
    give(own_a, 0, 0, 0)
    give(own_b, 0, 0, 1)


def contract(steps, direct, got, w):
    vmem = pl.BlockSpec(memory_space=pltpu.VMEM)
    hbm = pl.BlockSpec(memory_space=pltpu.HBM)
    row_count = w.shape[0]
    half = row_count // X // 2
    slots = slots_of(steps)
    most = GROUP * slots + 2 * steps * WIDE
    one = jax.ShapeDtypeStruct((steps * half, 2 * TILE), jnp.float32)
    two = jax.ShapeDtypeStruct((2 * steps * half, 2 * TILE), jnp.float32)

    outs = [two] * X if direct else [one, one, two, two, one, one]

    def kernel(*refs):
        contract_kernel(steps, direct, *refs)

    return pl.pallas_call(
        kernel,
        out_shape=outs,
        in_specs=[hbm, hbm],
        out_specs=[vmem] * len(outs),
        scratch_shapes=[
            pltpu.VMEM((steps * GROUP + 1, CAP * TILE, TILE), jnp.bfloat16),
            pltpu.VMEM((2 * steps, row_count, TILE), jnp.float32),
            pltpu.VMEM((DEPTH, row_count, WIDE * TILE), jnp.bfloat16),
            pltpu.VMEM((GROUP, META, TILE), jnp.bfloat16),
            pltpu.VMEM((GROUP, TILE), jnp.int32),
            pltpu.SMEM((GROUP, TILE), jnp.int32),
            pltpu.SMEM((most,), jnp.int32),
            pltpu.SemaphoreType.DMA((2 + steps,)),
            pltpu.SemaphoreType.DMA((DEPTH, WIDE)),
        ],
        compiler_params=pltpu.CompilerParams(vmem_limit_bytes=56 << 20),
        cost_estimate=pl.CostEstimate(flops=1 << 20, bytes_accessed=1 << 20, transcendentals=0),
        name="contract",
    )(got, w)


def local(t2_tiles, kc_tile, jb_tile, tile_owner, w_slices):
    half = w_slices.shape[0] // X // 2
    up_x = [(i, (i + 1) % X) for i in range(X)]
    down_x = [(i, (i - 1) % X) for i in range(X)]
    names = tile_owner.reshape(-1)
    gots = [
        lax.all_to_all(sent, ("zl", "y", "k"), split_axis=0, concat_axis=0, tiled=True)
        for sent in route(kc_tile, jb_tile, names, t2_tiles)
    ]

    def join(steps, sums):
        own_a, own_b, up, down, next_b, last_a = sums
        cut = steps * half
        from_low = lax.ppermute(up, "x", up_x)
        from_high = lax.ppermute(down, "x", down_x)
        next_b, last_a = next_b + from_low[:cut], last_a + from_high[:cut]
        return next_b, last_a, own_a, own_b, from_low, from_high

    def blocks(steps, joined):
        next_b, last_a, own_a, own_b, from_low, from_high = joined
        from_low_b = lax.ppermute(next_b, "x", up_x)
        from_high_a = lax.ppermute(last_a, "x", down_x)
        done = []
        for s in range(steps):
            here = slice(s * half, (s + 1) * half)
            there = slice((steps + s) * half, (steps + s + 1) * half)
            block_a = own_a[here] + from_low[there] + from_high_a[here]
            block_b = own_b[here] + from_high[there] + from_low_b[here]
            done.append(jnp.concatenate([block_a, block_b], axis=0))
        return done

    def send(block, away):
        if not away:
            return block
        return lax.ppermute(block, "zh", [(i, (i + away) % HIGH) for i in range(HIGH)])

    steps = CHUNKS[0]
    first = contract(steps, False, gots[0], w_slices)
    own, after, far, behind = contract(CHUNKS[1], True, gots[1], w_slices)
    first = join(steps, first)
    low_b, high_a, after, behind, far = lax.optimization_barrier((*first[:2], after, behind, far))
    early = blocks(steps, (low_b, high_a, *first[2:]))
    parts = [send(b, ORDER[s]) for s, b in enumerate(early)]
    parts += [own, lax.ppermute(after, "x", up_x), lax.ppermute(behind, "x", down_x)]
    parts += [lax.ppermute(far, "x", [(i, (i + 2) % X) for i in range(X)])]
    return sum(parts[1:], parts[0]).astype(jnp.bfloat16)


def solution(mesh):
    every = ("zh", "zl", "y", "k", "x")
    fine = Mesh(mesh.devices.reshape(HIGH, LOW, Y, K, X), every)
    return jax.shard_map(
        local,
        mesh=fine,
        in_specs=(
            P(every, None, None),
            P(every),
            P(every),
            P(every, None),
            P(None, "x"),
        ),
        out_specs=P("x", every[:4]),
        check_vma=False,
    )
```

```python
import jax
import jax.numpy as jnp
from jax import lax
from jax.experimental import pallas as pl
from jax.experimental.pallas import tpu as pltpu
from jax.sharding import Mesh
from jax.sharding import PartitionSpec as P

HIGH, LOW, Y, K, X = 4, 2, 4, 2, 4
GROUP = LOW * Y * K
CAP = 3
TILE = 128
META = 16
DEPTH = 4
WIDE = 4
PARTS = 4
ORDER = (2, 1, 3, 0)
CHUNKS = (3, 1)
FIRST = (0, 3)


def slots_of(steps):
    return steps * CAP


def block_of(steps):
    return slots_of(steps) * TILE + META


def route_kernel(kc, jb, owner, tiles, *rest):
    sends, scratch = rest[: len(CHUNKS)], rest[len(CHUNKS) :]
    kc_s, jb_s, owner_s, counts, codes, metas, stage, kind_sem, stage_sem, meta_sem, sem = scratch
    held = tiles.shape[0]
    part = held // PARTS

    def load_part(p):
        some = pl.ds(p * part, part)
        return pltpu.make_async_copy(tiles.at[some], stage.at[some], stage_sem.at[p])

    loads = [
        pltpu.make_async_copy(a, b, kind_sem.at[i])
        for i, (a, b) in enumerate(((kc, kc_s), (jb, jb_s), (owner, owner_s)))
    ]
    for load in loads:
        load.start()
    for p in range(PARTS):
        load_part(p).start()

    def clear(o, carry):
        counts[o] = 0
        return carry

    lax.fori_loop(0, HIGH * GROUP, clear, 0)
    codes[...] = jnp.full(codes.shape, -1.0, jnp.float32)
    lane = lax.broadcasted_iota(jnp.int32, (1, TILE), 1)
    high = lax.axis_index("zh")
    for load in loads:
        load.wait()

    def one(i, carry):
        name = owner_s[i]
        away = (lax.shift_right_logical(name, 4) - high) & (HIGH - 1)
        step = jnp.int32(0)
        for s in range(1, HIGH):
            step = jnp.where(away == ORDER[s], s, step)
        rank = counts[name]
        counts[name] = rank + 1
        dest = name & (GROUP - 1)
        for c, send in enumerate(sends):

            @pl.when((step >= FIRST[c]) & (step < FIRST[c] + CHUNKS[c]))
            def _():
                row = pl.multiple_of(((step - FIRST[c]) * CAP + rank) * TILE, TILE)
                pltpu.make_async_copy(stage.at[i], send.at[dest, pl.ds(row, TILE), :], sem).start()

        line = pl.ds(dest, 1)
        code = (kc_s[i] * 2 + jb_s[i]).astype(jnp.float32)
        codes[line, :] = jnp.where(lane == step * CAP + rank, code, codes[line, :])
        return carry

    for p in range(PARTS):
        load_part(p).wait()
        lax.fori_loop(p * part, (p + 1) * part, one, 0)
    copies = []
    for c, send in enumerate(sends):
        found = codes[...]
        if FIRST[c]:
            found = pltpu.roll(found, TILE - FIRST[c] * CAP, axis=1)
        metas[c] = jnp.broadcast_to(found[:, None, :], (GROUP, META, TILE)).astype(metas.dtype)
        there = send.at[:, pl.ds(slots_of(CHUNKS[c]) * TILE, META), :]
        copies.append(pltpu.make_async_copy(metas.at[c], there, meta_sem.at[c]))
    for copy in copies:
        copy.start()
    for copy in copies:
        copy.wait()
    pltpu.make_async_copy(stage, stage, sem).wait()


def route(kc, jb, owner, tiles):
    hbm = pl.BlockSpec(memory_space=pltpu.HBM)
    held = tiles.shape[0]
    return pl.pallas_call(
        route_kernel,
        out_shape=[jax.ShapeDtypeStruct((GROUP, block_of(n), TILE), tiles.dtype) for n in CHUNKS],
        in_specs=[hbm] * 4,
        out_specs=[hbm] * len(CHUNKS),
        scratch_shapes=[
            pltpu.SMEM((held,), jnp.int32),
            pltpu.SMEM((held,), jnp.int32),
            pltpu.SMEM((held,), jnp.int32),
            pltpu.SMEM((HIGH * GROUP,), jnp.int32),
            pltpu.VMEM((GROUP, TILE), jnp.float32),
            pltpu.VMEM((len(CHUNKS), GROUP, META, TILE), tiles.dtype),
            pltpu.VMEM(tiles.shape, tiles.dtype),
            pltpu.SemaphoreType.DMA((3,)),
            pltpu.SemaphoreType.DMA((PARTS,)),
            pltpu.SemaphoreType.DMA((len(CHUNKS),)),
            pltpu.SemaphoreType.DMA,
        ],
        compiler_params=pltpu.CompilerParams(vmem_limit_bytes=60 << 20),
        cost_estimate=pl.CostEstimate(flops=0, bytes_accessed=8 << 20, transcendentals=0),
        name="route",
    )(kc, jb, owner, tiles)


def contract_kernel(steps, direct, got, w, *rest):
    many = 4 if direct else 6
    outs = rest[:many]
    tiles, total, held, codes_b, codes_v, codes, work, sems, w_sem = rest[many:]
    row_count = w.shape[0]
    half = row_count // X // 2
    deep = CAP * TILE
    metas = pltpu.make_async_copy(got.at[:, pl.ds(got.shape[1] - META, META), :], codes_b, sems.at[0])
    metas.start()

    def arrive(s):
        here = got.at[:, pl.ds(s * deep, deep), :]
        return pltpu.make_async_copy(here, tiles.at[pl.ds(s * GROUP, GROUP)], sems.at[2 + s])

    for s in range(steps):
        arrive(s).start()
    tiles[steps * GROUP] = jnp.zeros((deep, TILE), tiles.dtype)
    metas.wait()
    codes_v[...] = codes_b[...][:, 0, :].astype(jnp.float32).astype(jnp.int32)
    copy = pltpu.make_async_copy(codes_v, codes, sems.at[1])
    copy.start()
    total[...] = jnp.zeros_like(total)
    copy.wait()

    def fetch(i, b, side):
        start = pl.multiple_of(lax.shift_right_logical(work[WIDE * i + side], 10) * TILE, TILE)
        return pltpu.make_async_copy(
            w.at[:, pl.ds(start, TILE)],
            held.at[b, :, pl.ds(side * TILE, TILE)],
            w_sem.at[b, side],
        )

    def fetch_first(least, most):
        for b in range(DEPTH):

            @pl.when((b >= least) & (b < most))
            def _():
                for side in range(WIDE):
                    fetch(b, b, side).start()

    count = jnp.int32(0)
    bounds = [jnp.int32(0)]
    for which in range(2 * steps):
        for j in range(GROUP):
            for rank in range(CAP):
                code = codes[j, which // 2 * CAP + rank]
                place = (which // 2 * GROUP + j) * 4 + rank
                work[count] = lax.shift_left(lax.shift_right_arithmetic(code, 1), 10) + place
                count = count + jnp.where((code >= 0) & ((code & 1) == which % 2), 1, 0)
        for _ in range(WIDE - 1):
            work[count] = steps * GROUP * 4
            count = count + jnp.where(lax.rem(count, WIDE) > 0, 1, 0)
        bounds.append(lax.div(count, WIDE))
        if which == 1:
            fetch_first(0, bounds[2])
    bunches = bounds[-1]
    if steps > 1:
        fetch_first(bounds[2], bunches)

    def picked(i, side):
        place = work[WIDE * i + side] & 1023
        row = pl.multiple_of((place & 3) * TILE, TILE)
        return tiles[lax.shift_right_logical(place, 2), pl.ds(row, TILE), :]

    for s in range(steps):
        arrive(s).wait()

        def one(i, carry, s=s):
            b = lax.rem(i, DEPTH)
            for side in range(WIDE):
                fetch(i, b, side).wait()
            right = jnp.concatenate([picked(i, side) for side in range(WIDE)], axis=0)
            which = 2 * s + jnp.where(i >= bounds[2 * s + 1], 1, 0)
            total[which] += jnp.dot(held[b], right, preferred_element_type=jnp.float32)

            @pl.when(i + DEPTH < bunches)
            def _():
                for side in range(WIDE):
                    fetch(i + DEPTH, b, side).start()

            return carry

        lax.fori_loop(bounds[2 * s], bounds[2 * s + 2], one, 0)
    x = lax.axis_index("x")

    def give(ref, at, away, side):
        first = lax.rem(x + away, X) * (2 * half) + side * half
        first = pl.multiple_of(first, half)
        for s in range(steps):
            for j in range(2):
                ref[at + s * half : at + (s + 1) * half, j * TILE : (j + 1) * TILE] = total[
                    s * 2 + j, pl.ds(first, half), :
                ]

    if direct:
        for away in range(X):
            give(outs[away], 0, away, 0)
            give(outs[away], steps * half, away, 1)
        return
    own_a, own_b, up, down, next_b, last_a = outs
    give(up, 0, 2, 1)
    give(up, steps * half, 1, 0)
    give(down, 0, 2, 0)
    give(down, steps * half, 3, 1)
    give(next_b, 0, 1, 1)
    give(last_a, 0, 3, 0)
    give(own_a, 0, 0, 0)
    give(own_b, 0, 0, 1)


def contract(steps, direct, got, w):
    vmem = pl.BlockSpec(memory_space=pltpu.VMEM)
    hbm = pl.BlockSpec(memory_space=pltpu.HBM)
    row_count = w.shape[0]
    half = row_count // X // 2
    slots = slots_of(steps)
    most = GROUP * slots + 2 * steps * WIDE
    one = jax.ShapeDtypeStruct((steps * half, 2 * TILE), jnp.float32)
    two = jax.ShapeDtypeStruct((2 * steps * half, 2 * TILE), jnp.float32)

    outs = [two] * X if direct else [one, one, two, two, one, one]

    def kernel(*refs):
        contract_kernel(steps, direct, *refs)

    return pl.pallas_call(
        kernel,
        out_shape=outs,
        in_specs=[hbm, hbm],
        out_specs=[vmem] * len(outs),
        scratch_shapes=[
            pltpu.VMEM((steps * GROUP + 1, CAP * TILE, TILE), jnp.bfloat16),
            pltpu.VMEM((2 * steps, row_count, TILE), jnp.float32),
            pltpu.VMEM((DEPTH, row_count, WIDE * TILE), jnp.bfloat16),
            pltpu.VMEM((GROUP, META, TILE), jnp.bfloat16),
            pltpu.VMEM((GROUP, TILE), jnp.int32),
            pltpu.SMEM((GROUP, TILE), jnp.int32),
            pltpu.SMEM((most,), jnp.int32),
            pltpu.SemaphoreType.DMA((2 + steps,)),
            pltpu.SemaphoreType.DMA((DEPTH, WIDE)),
        ],
        compiler_params=pltpu.CompilerParams(vmem_limit_bytes=56 << 20),
        cost_estimate=pl.CostEstimate(flops=1 << 20, bytes_accessed=1 << 20, transcendentals=0),
        name="contract",
    )(got, w)


def local(t2_tiles, kc_tile, jb_tile, tile_owner, w_slices):
    half = w_slices.shape[0] // X // 2
    up_x = [(i, (i + 1) % X) for i in range(X)]
    down_x = [(i, (i - 1) % X) for i in range(X)]
    names = tile_owner.reshape(-1)
    gots = [
        lax.all_to_all(sent, ("zl", "y", "k"), split_axis=0, concat_axis=0, tiled=True)
        for sent in route(kc_tile, jb_tile, names, t2_tiles)
    ]

    def join(steps, sums):
        own_a, own_b, up, down, next_b, last_a = sums
        cut = steps * half
        from_low = lax.ppermute(up, "x", up_x)
        from_high = lax.ppermute(down, "x", down_x)
        next_b, last_a = next_b + from_low[:cut], last_a + from_high[:cut]
        return next_b, last_a, own_a, own_b, from_low, from_high

    def blocks(steps, joined):
        next_b, last_a, own_a, own_b, from_low, from_high = joined
        from_low_b = lax.ppermute(next_b, "x", up_x)
        from_high_a = lax.ppermute(last_a, "x", down_x)
        done = []
        for s in range(steps):
            here = slice(s * half, (s + 1) * half)
            there = slice((steps + s) * half, (steps + s + 1) * half)
            block_a = own_a[here] + from_low[there] + from_high_a[here]
            block_b = own_b[here] + from_high[there] + from_low_b[here]
            done.append(jnp.concatenate([block_a, block_b], axis=0))
        return done

    def send(block, away):
        if not away:
            return block
        return lax.ppermute(block, "zh", [(i, (i + away) % HIGH) for i in range(HIGH)])

    steps = CHUNKS[0]
    first = contract(steps, False, gots[0], w_slices)
    own, after, far, behind = contract(CHUNKS[1], True, gots[1], w_slices)
    *first, next_b, last_a = first
    next_b, last_a, own = lax.optimization_barrier((next_b, last_a, own))
    first = join(steps, (*first, next_b, last_a))
    early = blocks(steps, first)
    after, behind, far, *early = lax.optimization_barrier((after, behind, far, *early))
    parts = [send(b, ORDER[s]) for s, b in enumerate(early)]
    parts += [own, lax.ppermute(after, "x", up_x), lax.ppermute(behind, "x", down_x)]
    parts += [lax.ppermute(far, "x", [(i, (i + 2) % X) for i in range(X)])]
    return sum(parts[1:], parts[0]).astype(jnp.bfloat16)


def solution(mesh):
    every = ("zh", "zl", "y", "k", "x")
    fine = Mesh(mesh.devices.reshape(HIGH, LOW, Y, K, X), every)
    return jax.shard_map(
        local,
        mesh=fine,
        in_specs=(
            P(every, None, None),
            P(every),
            P(every),
            P(every, None),
            P(None, "x"),
        ),
        out_specs=P("x", every[:4]),
        check_vma=False,
    )
```

```python
import jax
import jax.numpy as jnp
from jax import lax
from jax.experimental import pallas as pl
from jax.experimental.pallas import tpu as pltpu
from jax.sharding import Mesh
from jax.sharding import PartitionSpec as P

HIGH, LOW, Y, K, X = 4, 2, 4, 2, 4
GROUP = LOW * Y * K
CAP = 3
TILE = 128
META = 16
DEPTH = 4
WIDE = 4
PARTS = 4
ORDER = (1, 3, 2, 0)
CHUNKS = (3, 1)
FIRST = (0, 3)


def slots_of(steps):
    return steps * CAP


def block_of(steps):
    return slots_of(steps) * TILE + META


def route_kernel(kc, jb, owner, tiles, *rest):
    sends, scratch = rest[: len(CHUNKS)], rest[len(CHUNKS) :]
    kc_s, jb_s, owner_s, counts, codes, metas, stage, kind_sem, stage_sem, meta_sem, sem = scratch
    held = tiles.shape[0]
    part = held // PARTS

    def load_part(p):
        some = pl.ds(p * part, part)
        return pltpu.make_async_copy(tiles.at[some], stage.at[some], stage_sem.at[p])

    loads = [
        pltpu.make_async_copy(a, b, kind_sem.at[i])
        for i, (a, b) in enumerate(((kc, kc_s), (jb, jb_s), (owner, owner_s)))
    ]
    for load in loads:
        load.start()
    for p in range(PARTS):
        load_part(p).start()

    def clear(o, carry):
        counts[o] = 0
        return carry

    lax.fori_loop(0, HIGH * GROUP, clear, 0)
    codes[...] = jnp.full(codes.shape, -1.0, jnp.float32)
    lane = lax.broadcasted_iota(jnp.int32, (1, TILE), 1)
    high = lax.axis_index("zh")
    for load in loads:
        load.wait()

    def one(i, carry):
        name = owner_s[i]
        away = (lax.shift_right_logical(name, 4) - high) & (HIGH - 1)
        step = jnp.int32(0)
        for s in range(1, HIGH):
            step = jnp.where(away == ORDER[s], s, step)
        rank = counts[name]
        counts[name] = rank + 1
        dest = name & (GROUP - 1)
        for c, send in enumerate(sends):

            @pl.when((step >= FIRST[c]) & (step < FIRST[c] + CHUNKS[c]))
            def _():
                row = pl.multiple_of(((step - FIRST[c]) * CAP + rank) * TILE, TILE)
                pltpu.make_async_copy(stage.at[i], send.at[dest, pl.ds(row, TILE), :], sem).start()

        line = pl.ds(dest, 1)
        code = (kc_s[i] * 2 + jb_s[i]).astype(jnp.float32)
        codes[line, :] = jnp.where(lane == step * CAP + rank, code, codes[line, :])
        return carry

    for p in range(PARTS):
        load_part(p).wait()
        lax.fori_loop(p * part, (p + 1) * part, one, 0)
    copies = []
    for c, send in enumerate(sends):
        found = codes[...]
        if FIRST[c]:
            found = pltpu.roll(found, TILE - FIRST[c] * CAP, axis=1)
        metas[c] = jnp.broadcast_to(found[:, None, :], (GROUP, META, TILE)).astype(metas.dtype)
        there = send.at[:, pl.ds(slots_of(CHUNKS[c]) * TILE, META), :]
        copies.append(pltpu.make_async_copy(metas.at[c], there, meta_sem.at[c]))
    for copy in copies:
        copy.start()
    for copy in copies:
        copy.wait()
    pltpu.make_async_copy(stage, stage, sem).wait()


def route(kc, jb, owner, tiles):
    hbm = pl.BlockSpec(memory_space=pltpu.HBM)
    held = tiles.shape[0]
    return pl.pallas_call(
        route_kernel,
        out_shape=[jax.ShapeDtypeStruct((GROUP, block_of(n), TILE), tiles.dtype) for n in CHUNKS],
        in_specs=[hbm] * 4,
        out_specs=[hbm] * len(CHUNKS),
        scratch_shapes=[
            pltpu.SMEM((held,), jnp.int32),
            pltpu.SMEM((held,), jnp.int32),
            pltpu.SMEM((held,), jnp.int32),
            pltpu.SMEM((HIGH * GROUP,), jnp.int32),
            pltpu.VMEM((GROUP, TILE), jnp.float32),
            pltpu.VMEM((len(CHUNKS), GROUP, META, TILE), tiles.dtype),
            pltpu.VMEM(tiles.shape, tiles.dtype),
            pltpu.SemaphoreType.DMA((3,)),
            pltpu.SemaphoreType.DMA((PARTS,)),
            pltpu.SemaphoreType.DMA((len(CHUNKS),)),
            pltpu.SemaphoreType.DMA,
        ],
        compiler_params=pltpu.CompilerParams(vmem_limit_bytes=60 << 20),
        cost_estimate=pl.CostEstimate(flops=0, bytes_accessed=8 << 20, transcendentals=0),
        name="route",
    )(kc, jb, owner, tiles)


def contract_kernel(steps, direct, got, w, *rest):
    many = 4 if direct else 6
    outs = rest[:many]
    tiles, total, held, codes_b, codes_v, codes, work, sems, w_sem = rest[many:]
    row_count = w.shape[0]
    half = row_count // X // 2
    deep = CAP * TILE
    metas = pltpu.make_async_copy(got.at[:, pl.ds(got.shape[1] - META, META), :], codes_b, sems.at[0])
    metas.start()

    def arrive(s):
        here = got.at[:, pl.ds(s * deep, deep), :]
        return pltpu.make_async_copy(here, tiles.at[pl.ds(s * GROUP, GROUP)], sems.at[2 + s])

    for s in range(steps):
        arrive(s).start()
    tiles[steps * GROUP] = jnp.zeros((deep, TILE), tiles.dtype)
    metas.wait()
    codes_v[...] = codes_b[...][:, 0, :].astype(jnp.float32).astype(jnp.int32)
    copy = pltpu.make_async_copy(codes_v, codes, sems.at[1])
    copy.start()
    total[...] = jnp.zeros_like(total)
    copy.wait()

    def fetch(i, b, side):
        start = pl.multiple_of(lax.shift_right_logical(work[WIDE * i + side], 10) * TILE, TILE)
        return pltpu.make_async_copy(
            w.at[:, pl.ds(start, TILE)],
            held.at[b, :, pl.ds(side * TILE, TILE)],
            w_sem.at[b, side],
        )

    def fetch_first(least, most):
        for b in range(DEPTH):

            @pl.when((b >= least) & (b < most))
            def _():
                for side in range(WIDE):
                    fetch(b, b, side).start()

    count = jnp.int32(0)
    bounds = [jnp.int32(0)]
    for which in range(2 * steps):
        for j in range(GROUP):
            for rank in range(CAP):
                code = codes[j, which // 2 * CAP + rank]
                place = (which // 2 * GROUP + j) * 4 + rank
                work[count] = lax.shift_left(lax.shift_right_arithmetic(code, 1), 10) + place
                count = count + jnp.where((code >= 0) & ((code & 1) == which % 2), 1, 0)
        for _ in range(WIDE - 1):
            work[count] = steps * GROUP * 4
            count = count + jnp.where(lax.rem(count, WIDE) > 0, 1, 0)
        bounds.append(lax.div(count, WIDE))
        if which == 1:
            fetch_first(0, bounds[2])
    bunches = bounds[-1]
    if steps > 1:
        fetch_first(bounds[2], bunches)

    def picked(i, side):
        place = work[WIDE * i + side] & 1023
        row = pl.multiple_of((place & 3) * TILE, TILE)
        return tiles[lax.shift_right_logical(place, 2), pl.ds(row, TILE), :]

    for s in range(steps):
        arrive(s).wait()

        def one(i, carry, s=s):
            b = lax.rem(i, DEPTH)
            for side in range(WIDE):
                fetch(i, b, side).wait()
            right = jnp.concatenate([picked(i, side) for side in range(WIDE)], axis=0)
            which = 2 * s + jnp.where(i >= bounds[2 * s + 1], 1, 0)
            total[which] += jnp.dot(held[b], right, preferred_element_type=jnp.float32)

            @pl.when(i + DEPTH < bunches)
            def _():
                for side in range(WIDE):
                    fetch(i + DEPTH, b, side).start()

            return carry

        lax.fori_loop(bounds[2 * s], bounds[2 * s + 2], one, 0)
    x = lax.axis_index("x")

    def give(ref, at, away, side):
        first = lax.rem(x + away, X) * (2 * half) + side * half
        first = pl.multiple_of(first, half)
        for s in range(steps):
            for j in range(2):
                ref[at + s * half : at + (s + 1) * half, j * TILE : (j + 1) * TILE] = total[
                    s * 2 + j, pl.ds(first, half), :
                ]

    if direct:
        for away in range(X):
            give(outs[away], 0, away, 0)
            give(outs[away], steps * half, away, 1)
        return
    own_a, own_b, up, down, next_b, last_a = outs
    give(up, 0, 2, 1)
    give(up, steps * half, 1, 0)
    give(down, 0, 2, 0)
    give(down, steps * half, 3, 1)
    give(next_b, 0, 1, 1)
    give(last_a, 0, 3, 0)
    give(own_a, 0, 0, 0)
    give(own_b, 0, 0, 1)


def contract(steps, direct, got, w):
    vmem = pl.BlockSpec(memory_space=pltpu.VMEM)
    hbm = pl.BlockSpec(memory_space=pltpu.HBM)
    row_count = w.shape[0]
    half = row_count // X // 2
    slots = slots_of(steps)
    most = GROUP * slots + 2 * steps * WIDE
    one = jax.ShapeDtypeStruct((steps * half, 2 * TILE), jnp.float32)
    two = jax.ShapeDtypeStruct((2 * steps * half, 2 * TILE), jnp.float32)

    outs = [two] * X if direct else [one, one, two, two, one, one]

    def kernel(*refs):
        contract_kernel(steps, direct, *refs)

    return pl.pallas_call(
        kernel,
        out_shape=outs,
        in_specs=[hbm, hbm],
        out_specs=[vmem] * len(outs),
        scratch_shapes=[
            pltpu.VMEM((steps * GROUP + 1, CAP * TILE, TILE), jnp.bfloat16),
            pltpu.VMEM((2 * steps, row_count, TILE), jnp.float32),
            pltpu.VMEM((DEPTH, row_count, WIDE * TILE), jnp.bfloat16),
            pltpu.VMEM((GROUP, META, TILE), jnp.bfloat16),
            pltpu.VMEM((GROUP, TILE), jnp.int32),
            pltpu.SMEM((GROUP, TILE), jnp.int32),
            pltpu.SMEM((most,), jnp.int32),
            pltpu.SemaphoreType.DMA((2 + steps,)),
            pltpu.SemaphoreType.DMA((DEPTH, WIDE)),
        ],
        compiler_params=pltpu.CompilerParams(vmem_limit_bytes=56 << 20),
        cost_estimate=pl.CostEstimate(flops=1 << 20, bytes_accessed=1 << 20, transcendentals=0),
        name="contract",
    )(got, w)


def local(t2_tiles, kc_tile, jb_tile, tile_owner, w_slices):
    half = w_slices.shape[0] // X // 2
    up_x = [(i, (i + 1) % X) for i in range(X)]
    down_x = [(i, (i - 1) % X) for i in range(X)]
    names = tile_owner.reshape(-1)
    gots = [
        lax.all_to_all(sent, ("zl", "y", "k"), split_axis=0, concat_axis=0, tiled=True)
        for sent in route(kc_tile, jb_tile, names, t2_tiles)
    ]

    def join(steps, sums):
        own_a, own_b, up, down, next_b, last_a = sums
        cut = steps * half
        from_low = lax.ppermute(up, "x", up_x)
        from_high = lax.ppermute(down, "x", down_x)
        next_b, last_a = next_b + from_low[:cut], last_a + from_high[:cut]
        return next_b, last_a, own_a, own_b, from_low, from_high

    def blocks(steps, joined):
        next_b, last_a, own_a, own_b, from_low, from_high = joined
        from_low_b = lax.ppermute(next_b, "x", up_x)
        from_high_a = lax.ppermute(last_a, "x", down_x)
        done = []
        for s in range(steps):
            here = slice(s * half, (s + 1) * half)
            there = slice((steps + s) * half, (steps + s + 1) * half)
            block_a = own_a[here] + from_low[there] + from_high_a[here]
            block_b = own_b[here] + from_high[there] + from_low_b[here]
            done.append(jnp.concatenate([block_a, block_b], axis=0))
        return done

    def send(block, away):
        if not away:
            return block
        return lax.ppermute(block, "zh", [(i, (i + away) % HIGH) for i in range(HIGH)])

    steps = CHUNKS[0]
    first = contract(steps, False, gots[0], w_slices)
    own, after, far, behind = contract(CHUNKS[1], True, gots[1], w_slices)
    *first, next_b, last_a = first
    next_b, last_a, own = lax.optimization_barrier((next_b, last_a, own))
    first = join(steps, (*first, next_b, last_a))
    early = blocks(steps, first)
    after, behind, far, *early = lax.optimization_barrier((after, behind, far, *early))
    parts = [send(b, ORDER[s]) for s, b in enumerate(early)]
    parts += [own, lax.ppermute(after, "x", up_x), lax.ppermute(behind, "x", down_x)]
    parts += [lax.ppermute(far, "x", [(i, (i + 2) % X) for i in range(X)])]
    return sum(parts[1:], parts[0]).astype(jnp.bfloat16)


def solution(mesh):
    every = ("zh", "zl", "y", "k", "x")
    fine = Mesh(mesh.devices.reshape(HIGH, LOW, Y, K, X), every)
    return jax.shard_map(
        local,
        mesh=fine,
        in_specs=(
            P(every, None, None),
            P(every),
            P(every),
            P(every, None),
            P(None, "x"),
        ),
        out_specs=P("x", every[:4]),
        check_vma=False,
    )
```
